32 devices in a mesh: head: 1, seq: 32 (over z, y, x, core).
Axes of the slice: x: 2, y: 2, z: 4, core: 2. Of those that a mesh axis runs over, the one named last changes fastest.
Arguments:
- query_rows: bfloat16 [8, 16384, 512], P('head', 'seq'), may hold values from -16 to 16
- key_rows: bfloat16 [8, 16384, 512], P('head', 'seq'), may hold values from -16 to 16
- value_rows: bfloat16 [8, 16384, 512], P('head', 'seq'), may hold values from -6 to 6
- step_rate: float32 [8, 16384], P('head', 'seq'), may hold values from 0.15 to 162
- doc_start: int32 [16384], P('seq'), may hold values from 0 to 16383, as said below
- speech_flag: int32 [16384], P('seq'), may hold values 0 or 1
- w_gate: bfloat16 [8, 512, 512], P('head'), may hold values from -0.25 to 0.25
- w_up: bfloat16 [8, 512, 512], P('head'), may hold values from -0.25 to 0.25
- w_down: bfloat16 [8, 512, 512], P('head'), may hold values from -0.25 to 0.25
- w_cond: bfloat16 [4096, 512], P('head'), may hold values from -0.09375 to 0.09375
Outputs:
- mixed: bfloat16 [8, 16384, 512], P('head', 'seq')
- cond: bfloat16 [32, 512, 512], P('seq', 'head')
The draws below stay inside these ranges and needn't reach their ends.
Inputs may be any that keep to these rules, and one draw needn't show every extreme that they name: doc_start[p] is the position of the first token of the document holding token p: at most p, never falling along the sequence, and doc_start[q] = q wherever a document begins; the last token begins a document of its own.
All inputs are finite; a program needn't handle non-finite values. No bound on the sum of `speech_flag` on one device may be relied on, other than what follows from the above.
Results may differ from the reference program's by a relative error of at most 0.015.
Values may be sent and summed in bfloat16 or wider, within the bound.
A program may use at most 128 MiB of HBM per device.

```python
import math
import jax
import jax.numpy as jnp
from jax import lax

HEADS = 8
HD = 512
COND = 512
WIN = 512
TOK_DEV = 512
TOKENS = 16384
UPDATE_TOK = 8192
WIDTH = 4096
N_SEQ = 32


def query_key_pair(key):
    base_key = jax.random.fold_in(key, 7)
    keys_all = jax.random.split(base_key, 2)
    query_base = jnp.clip(jax.random.normal(keys_all[0], (HEADS, TOKENS, HD), jnp.float32), -6.0, 6.0)
    key_base = jnp.clip(jax.random.normal(keys_all[1], (HEADS, TOKENS, HD), jnp.float32), -6.0, 6.0)
    return (query_base, key_base)


def draw_query_rows(key, part):
    return query_key_pair(key)[0].astype(jnp.bfloat16)


def draw_key_rows(key, part):
    return query_key_pair(key)[1].astype(jnp.bfloat16)


def draw_step_rate(key, part):
    keys_all = jax.random.split(jax.random.fold_in(key, 11), 2)
    position = jnp.arange(TOKENS, dtype=jnp.float32) / TOKENS
    head_scale = jnp.exp(jax.random.uniform(keys_all[1], (HEADS, 1), jnp.float32, math.log(0.5), math.log(2.0)))
    ramp = jnp.exp(math.log(9.0) * position)
    jitter = jnp.exp(jax.random.uniform(keys_all[0], (HEADS, TOKENS), jnp.float32, math.log(0.3), math.log(3.0)))
    return (jitter * ramp[None, :] * head_scale).astype(jnp.float32)


def draw_doc_start(key, part):
    marks = jax.random.randint(jax.random.fold_in(key, 23), (TOKENS,), 0, 2 * WIN)
    position = jnp.arange(TOKENS, dtype=jnp.int32)
    begins = jnp.where((marks == 0) | (position == 0) | (position == TOKENS - 1), position, 0)
    return lax.cummax(begins, axis=0).astype(jnp.int32)


def place_ends(entries, key, smallest, largest):
    index_at = [jax.random.randint(jax.random.fold_in(key, axis), (), 0, length) for axis, length in enumerate(entries.shape)]
    main_axis = entries.shape.index(max(entries.shape))
    beside = index_at[:main_axis] + [(index_at[main_axis] + 1) % entries.shape[main_axis]] + index_at[main_axis + 1:]
    return entries.at[tuple(index_at)].set(smallest).at[tuple(beside)].set(largest)


def block_levels(own_key, shape, cuts, least, high):
    loudness, own = 1.0, jax.random.fold_in(own_key, 6)
    for dim, shards_of in cuts:
        draws = jnp.exp(jax.random.uniform(jax.random.fold_in(own, dim), (shards_of,), jnp.float32, least / len(cuts), high / len(cuts)))
        loudness = loudness * jnp.repeat(draws, shape[dim] // shards_of).reshape([-1 if axis == dim else 1 for axis in range(len(shape))])
    return loudness


def scatter_about(key, dims, spread, most, cuts=(), kind=jnp.bfloat16):
    entries = spread * jax.random.normal(key, dims, jnp.float32)
    if cuts:
        entries = entries * block_levels(key, dims, cuts, -0.22, 0.18)
    return jnp.clip(entries, -most, most).astype(kind)


def setup_inputs(seed: int = 0) -> dict:
    seeds = jax.random.split(jax.random.key(seed), 11)
    query_rows = draw_query_rows(jax.random.fold_in(seeds[10], 71), 0)
    key_rows = draw_key_rows(jax.random.fold_in(seeds[10], 71), 0)
    value_rows = scatter_about(seeds[2], (HEADS, TOKENS, HD), 1.0, 6.0, ((1, 32),))
    step_rate = draw_step_rate(jax.random.fold_in(seeds[10], 71), 0)
    doc_start = draw_doc_start(jax.random.fold_in(seeds[10], 71), 0)
    speech_flag = place_ends((jax.random.randint(seeds[5], (TOKENS,), 0, 2) < 1).astype(jnp.int32), jax.random.fold_in(seeds[5], 1), 0, 1)
    w_gate = scatter_about(seeds[6], (HEADS, HD, HD), HD ** -0.5, 0.25)
    w_up = scatter_about(seeds[7], (HEADS, HD, HD), HD ** -0.5, 0.25)
    w_down = scatter_about(seeds[8], (HEADS, HD, HD), HD ** -0.5, 0.25)
    w_cond = scatter_about(seeds[9], (WIDTH, COND), WIDTH ** -0.5, 0.09375)
    return {"query_rows": query_rows, "key_rows": key_rows, "value_rows": value_rows, "step_rate": step_rate, "doc_start": doc_start, "speech_flag": speech_flag, "w_gate": w_gate, "w_up": w_up, "w_down": w_down, "w_cond": w_cond}


eps_norm = 1e-06

def renormed(old_weight, summed, factor):
    old_f = old_weight.astype(jnp.float32)
    updated = old_f + summed * factor[:, None, None]
    old_norm = jnp.sqrt(lax.optimization_barrier(jnp.sum(old_f * old_f, axis=-1, keepdims=True)))
    new_norm = jnp.sqrt(lax.optimization_barrier(jnp.sum(updated * updated, axis=-1, keepdims=True)) + eps_norm)
    return (updated * (old_norm / new_norm)).astype(jnp.bfloat16)

def fast_apply(rows_in, weight_gate, weight_up, weight_down):
    gate_pre = jnp.einsum('htd,hrd->htr', rows_in.astype(jnp.float32), weight_gate.astype(jnp.float32))
    up_pre = jnp.einsum('htd,hrd->htr', rows_in.astype(jnp.float32), weight_up.astype(jnp.float32))
    hidden = (gate_pre * jax.nn.sigmoid(gate_pre) * up_pre).astype(jnp.bfloat16)
    return jnp.einsum('htr,hdr->htd', hidden.astype(jnp.float32), weight_down.astype(jnp.float32))

def reference(query_rows, key_rows, value_rows, step_rate, doc_start, speech_flag, w_gate, w_up, w_down, w_cond):
    block_rows = min(512, TOKENS)
    score_scale = 1.0 / math.sqrt(HD)

    def attend_head(operands):
        query_head, key_head, value_head = operands
        key_pad = jnp.concatenate([jnp.zeros((WIN, HD), key_head.dtype), key_head], axis=0)
        value_pad = jnp.concatenate([jnp.zeros((WIN, HD), value_head.dtype), value_head], axis=0)

        def one_block(row_start):
            query_blk = lax.dynamic_slice_in_dim(query_head, row_start, block_rows, 0)
            key_blk = lax.dynamic_slice_in_dim(key_pad, row_start, WIN + block_rows, 0)
            value_blk = lax.dynamic_slice_in_dim(value_pad, row_start, WIN + block_rows, 0)
            starts_doc = lax.dynamic_slice_in_dim(doc_start, row_start, block_rows, 0)
            pos_query = row_start + jnp.arange(block_rows, dtype=jnp.int32)
            pos_key = row_start - WIN + jnp.arange(WIN + block_rows, dtype=jnp.int32)
            allowed = (pos_key[None, :] <= pos_query[:, None]) & (pos_key[None, :] > pos_query[:, None] - WIN) & (pos_key[None, :] >= starts_doc[:, None])
            scores = jnp.dot(query_blk, key_blk.T, preferred_element_type=jnp.float32) * score_scale
            scores = jnp.where(allowed, scores, -1e+30)
            row_max = lax.optimization_barrier(jnp.max(scores, axis=-1, keepdims=True))
            expon = jnp.exp(scores - row_max)
            prob_bf = (expon / lax.optimization_barrier(jnp.sum(expon, axis=-1, keepdims=True))).astype(jnp.bfloat16)
            return jnp.dot(prob_bf, value_blk, preferred_element_type=jnp.float32)
        starts = jnp.arange(TOKENS // block_rows, dtype=jnp.int32) * block_rows
        return lax.map(one_block, starts).reshape(TOKENS, HD)
    attended = lax.map(attend_head, (query_rows, key_rows, value_rows))
    speech_on = speech_flag.astype(jnp.float32)
    key_first = key_rows[:, :UPDATE_TOK]
    scaled = (speech_on[None, :UPDATE_TOK, None] * step_rate[:, :UPDATE_TOK, None] * value_rows[:, :UPDATE_TOK].astype(jnp.float32)).astype(jnp.bfloat16)
    gate_pre = jnp.einsum('htd,hrd->htr', key_first.astype(jnp.float32), w_gate.astype(jnp.float32))
    up_pre = jnp.einsum('htd,hrd->htr', key_first.astype(jnp.float32), w_up.astype(jnp.float32))
    sigma = jax.nn.sigmoid(gate_pre)
    active = gate_pre * sigma
    hidden_zero = (active * up_pre).astype(jnp.bfloat16)
    back = jnp.einsum('htd,hdr->htr', scaled.astype(jnp.float32), w_down.astype(jnp.float32))
    grad_gate = (back * up_pre * sigma * (1.0 + gate_pre * (1.0 - sigma))).astype(jnp.bfloat16)
    grad_up = (back * active).astype(jnp.bfloat16)
    sum_gate = jnp.einsum('htr,htd->hrd', grad_gate.astype(jnp.float32), key_first.astype(jnp.float32))
    sum_up = jnp.einsum('htr,htd->hrd', grad_up.astype(jnp.float32), key_first.astype(jnp.float32))
    sum_down = jnp.einsum('htd,htr->hdr', scaled.astype(jnp.float32), hidden_zero.astype(jnp.float32))
    totals = lax.optimization_barrier(jnp.sum(step_rate[:, :UPDATE_TOK], axis=1))
    factor = 2.0 * UPDATE_TOK / (totals * math.sqrt(UPDATE_TOK * HD))
    new_gate = renormed(w_gate, sum_gate, factor)
    new_up = renormed(w_up, sum_up, factor)
    new_down = renormed(w_down, sum_down, factor)
    fast_first = fast_apply(query_rows[:, :UPDATE_TOK], w_gate, w_up, w_down)
    fast_second = fast_apply(query_rows[:, UPDATE_TOK:], new_gate, new_up, new_down)
    fast_out = jnp.concatenate([fast_first, fast_second], axis=1)
    mixed = (attended + fast_out).astype(jnp.bfloat16)
    cond_weight = w_cond.reshape(HEADS, HD, COND).astype(jnp.float32)
    projected = jnp.einsum('htd,hdc->tc', mixed.astype(jnp.float32), cond_weight)
    cond = (projected * speech_on[:, None]).astype(jnp.bfloat16).reshape(N_SEQ, TOK_DEV, COND)
    return (mixed, cond)
```

```python
import math

import jax
import jax.numpy as jnp
from jax import lax
from jax.sharding import PartitionSpec as P

WIN = 512


eps_norm = 1e-06


def passed_along(block, axis, distance):
    devices = range(lax.axis_size(axis))
    route = [(i - distance, i) for i in devices if i - distance in devices]
    return lax.ppermute(block, axis, route)


def renorm_rows(old_rows, summed, factor):
    old_f = old_rows.astype(jnp.float32)
    updated = old_f + summed.astype(jnp.float32) * factor[:, None]
    old_norm = jnp.sqrt(jnp.sum(old_f * old_f, axis=-1, keepdims=True))
    new_norm = jnp.sqrt(jnp.sum(updated * updated, axis=-1, keepdims=True) + eps_norm)
    return (updated * (old_norm / new_norm)).astype(jnp.bfloat16)


def half_total(rate, seq_count):
    half = seq_count // 2
    if half & (half - 1):
        in_first = lax.axis_index("seq") < half
        return lax.psum(jnp.where(in_first, rate, 0.0), "seq")
    step = 1
    while step < half:
        rate = rate + lax.ppermute(rate, "seq", [(i, i ^ step) for i in range(seq_count)])
        step *= 2
    return rate


def local(
    query_rows,
    key_rows,
    value_rows,
    step_rate,
    doc_start,
    speech_flag,
    w_gate,
    w_up,
    w_down,
    w_cond,
):
    head_local, tok_local, head_width = query_rows.shape
    cond_width = w_cond.shape[1]
    seq_count = lax.axis_size("seq")
    head_count = lax.axis_size("head")
    seq_index = lax.axis_index("seq")
    offset = seq_index * tok_local
    half_seq = seq_count // 2
    update_len = tok_local * half_seq
    in_first = seq_index < half_seq
    speech_on = speech_flag.astype(jnp.float32)
    prev_key, prev_value = passed_along((key_rows, value_rows), "seq", 1)
    score_scale = 1.0 / math.sqrt(head_width)
    groups = [list(range(half_seq)), list(range(half_seq, seq_count))]
    totals = half_total(jnp.sum(step_rate, axis=1), seq_count)

    scaled = (
        speech_on[None, :, None] * step_rate[:, :, None] * value_rows.astype(jnp.float32)
    ).astype(jnp.bfloat16)
    gate_pre = jnp.einsum("htd,hrd->htr", key_rows, w_gate, preferred_element_type=jnp.float32)
    up_pre = jnp.einsum("htd,hrd->htr", key_rows, w_up, preferred_element_type=jnp.float32)
    sigma = jax.nn.sigmoid(gate_pre)
    active = gate_pre * sigma
    hidden_zero = (active * up_pre).astype(jnp.bfloat16)
    back = jnp.einsum("htd,hdr->htr", scaled, w_down, preferred_element_type=jnp.float32)
    grad_gate = (back * up_pre * sigma * (1.0 + gate_pre * (1.0 - sigma))).astype(jnp.bfloat16)
    grad_up = (back * active).astype(jnp.bfloat16)

    flat = (head_local * head_width, head_width)
    half_index = lax.rem(seq_index, half_seq)
    share = flat[0] // half_seq

    def own_rows(rows):
        return lax.dynamic_slice_in_dim(rows, half_index * share, share, 0)

    def reduced(left, right):
        term = jnp.einsum("hta,htb->hab", left, right, preferred_element_type=jnp.float32)
        return term.astype(jnp.bfloat16).reshape(flat)

    def scattered(term):
        return lax.psum_scatter(
            term, "seq", scatter_dimension=0, axis_index_groups=groups, tiled=True
        )

    term_gate = reduced(grad_gate, key_rows)
    term_gate, prev_key, totals = lax.optimization_barrier((term_gate, prev_key, totals))
    sum_gate = scattered(term_gate)
    sum_up = scattered(reduced(grad_up, key_rows))
    term_down = reduced(scaled, hidden_zero)
    term_down, prev_value = lax.optimization_barrier((term_down, prev_value))
    sum_down = scattered(term_down)

    keys_all = jnp.concatenate([prev_key, key_rows], axis=1)
    values_all = jnp.concatenate([prev_value, value_rows], axis=1)
    pos_query = offset + jnp.arange(tok_local, dtype=jnp.int32)
    pos_key = offset - WIN + jnp.arange(WIN + tok_local, dtype=jnp.int32)
    allowed = (
        (pos_key[None, :] <= pos_query[:, None])
        & (pos_key[None, :] > pos_query[:, None] - WIN)
        & (pos_key[None, :] >= doc_start[:, None])
    )
    scores = (
        jnp.einsum("hqd,hkd->hqk", query_rows, keys_all, preferred_element_type=jnp.float32)
        * score_scale
    )
    scores = jnp.where(allowed[None], scores, -1e30)
    row_max = jnp.max(scores, axis=-1, keepdims=True)
    expon = jnp.exp(scores - row_max)
    prob_bf = (expon / jnp.sum(expon, axis=-1, keepdims=True)).astype(jnp.bfloat16)
    attended = jnp.einsum(
        "hqk,hkd->hqd", prob_bf, values_all, preferred_element_type=jnp.float32
    ).astype(jnp.bfloat16)

    sum_gate, attended = lax.optimization_barrier((sum_gate, attended))
    inner = 2.0 * update_len / (totals * math.sqrt(update_len * head_width))
    factor = own_rows(jnp.repeat(inner, head_width))

    def renewed(weight, summed):
        old = own_rows(weight.reshape(flat))
        sent = passed_along(renorm_rows(old, summed, factor), "seq", half_seq)
        return jnp.where(in_first, old, sent)

    def gathered(rows):
        whole = lax.all_gather(rows, "seq", axis=0, axis_index_groups=groups, tiled=True)
        return whole.reshape(head_local, head_width, head_width)

    rows_gate = renewed(w_gate, sum_gate)
    rows_gate, sum_up = lax.optimization_barrier((rows_gate, sum_up))
    use_gate = gathered(rows_gate)
    rows_up = renewed(w_up, sum_up)
    rows_up, sum_down = lax.optimization_barrier((rows_up, sum_down))
    use_up = gathered(rows_up)
    use_down = gathered(renewed(w_down, sum_down))

    query_gate = jnp.einsum("htd,hrd->htr", query_rows, use_gate, preferred_element_type=jnp.float32)
    query_up = jnp.einsum("htd,hrd->htr", query_rows, use_up, preferred_element_type=jnp.float32)
    query_hidden = (query_gate * jax.nn.sigmoid(query_gate) * query_up).astype(jnp.bfloat16)
    query_hidden, use_down = lax.optimization_barrier((query_hidden, use_down))
    fast_out = jnp.einsum(
        "htr,hdr->htd", query_hidden, use_down, preferred_element_type=jnp.float32
    )
    mixed = (attended + fast_out).astype(jnp.bfloat16)
    frame_rows = tok_local // head_count
    head_index = lax.axis_index("head")
    flag_rows = lax.dynamic_slice_in_dim(speech_on, head_index * frame_rows, frame_rows, 0)
    cond_weight = w_cond.reshape(head_local, head_width, cond_width)
    projected = lax.psum_scatter(
        jnp.einsum("htd,hdc->tc", mixed, cond_weight, preferred_element_type=jnp.float32).astype(
            jnp.bfloat16
        ),
        "head",
        scatter_dimension=0,
        tiled=True,
    ).astype(jnp.float32)
    cond = (projected * flag_rows[:, None]).astype(jnp.bfloat16)[None]
    return (mixed, cond)


def solution(mesh):
    placed = (
        P("head", "seq", None),
        P("head", "seq", None),
        P("head", "seq", None),
        P("head", "seq"),
        P("seq"),
        P("seq"),
        P("head", None, None),
        P("head", None, None),
        P("head", None, None),
        P("head", None),
    )
    return jax.shard_map(
        local,
        mesh=mesh,
        in_specs=placed,
        out_specs=(P("head", "seq", None), P("seq", "head", None)),
        check_vma=False,
    )
```

```python
import math

import jax
import jax.numpy as jnp
from jax import lax
from jax.sharding import PartitionSpec as P

WIN = 512


eps_norm = 1e-06


def passed_along(block, axis, distance):
    devices = range(lax.axis_size(axis))
    route = [(i - distance, i) for i in devices if i - distance in devices]
    return lax.ppermute(block, axis, route)


def renorm_rows(old_rows, summed, factor):
    old_f = old_rows.astype(jnp.float32)
    updated = old_f + summed.astype(jnp.float32) * factor[:, None]
    old_norm = jnp.sqrt(jnp.sum(old_f * old_f, axis=-1, keepdims=True))
    new_norm = jnp.sqrt(jnp.sum(updated * updated, axis=-1, keepdims=True) + eps_norm)
    return (updated * (old_norm / new_norm)).astype(jnp.bfloat16)


def swapped(block, step):
    route = [(i, i ^ step) for i in range(lax.axis_size("seq"))]
    return lax.ppermute(block, "seq", route)


def half_total(rate, steps):
    for step in steps:
        rate = rate + swapped(rate, step)
    return rate


def upper_side(step):
    return lax.rem(lax.axis_index("seq") // step, 2) == 1


def halved(rows, step):
    count = rows.shape[0] // 2
    upper = upper_side(step)
    low, high = rows[:count], rows[count:]
    kept = jnp.where(upper, high, low)
    came = swapped(jnp.where(upper, low, high), step)
    return (kept.astype(jnp.float32) + came.astype(jnp.float32)).astype(jnp.bfloat16)


def doubled(rows, step):
    upper = upper_side(step)
    came = swapped(rows, step)
    return jnp.concatenate([jnp.where(upper, came, rows), jnp.where(upper, rows, came)], axis=0)


def local(
    query_rows,
    key_rows,
    value_rows,
    step_rate,
    doc_start,
    speech_flag,
    w_gate,
    w_up,
    w_down,
    w_cond,
):
    head_local, tok_local, head_width = query_rows.shape
    cond_width = w_cond.shape[1]
    seq_count = lax.axis_size("seq")
    head_count = lax.axis_size("head")
    seq_index = lax.axis_index("seq")
    offset = seq_index * tok_local
    half_seq = seq_count // 2
    update_len = tok_local * half_seq
    in_first = seq_index < half_seq
    speech_on = speech_flag.astype(jnp.float32)
    prev_key, prev_value = passed_along((key_rows, value_rows), "seq", 1)
    score_scale = 1.0 / math.sqrt(head_width)
    steps = [1 << bit for bit in range(half_seq.bit_length() - 1)]
    near, far = steps[:1], steps[1:]
    turns = [near + far[turn:] + far[:turn] for turn in (0, 1, 2)]
    totals = half_total(jnp.sum(step_rate, axis=1), steps)

    scaled = (
        speech_on[None, :, None] * step_rate[:, :, None] * value_rows.astype(jnp.float32)
    ).astype(jnp.bfloat16)
    gate_pre = jnp.einsum("htd,hrd->htr", key_rows, w_gate, preferred_element_type=jnp.float32)
    up_pre = jnp.einsum("htd,hrd->htr", key_rows, w_up, preferred_element_type=jnp.float32)
    sigma = jax.nn.sigmoid(gate_pre)
    active = gate_pre * sigma
    hidden_zero = (active * up_pre).astype(jnp.bfloat16)
    back = jnp.einsum("htd,hdr->htr", scaled, w_down, preferred_element_type=jnp.float32)
    grad_gate = (back * up_pre * sigma * (1.0 + gate_pre * (1.0 - sigma))).astype(jnp.bfloat16)
    grad_up = (back * active).astype(jnp.bfloat16)

    flat = (head_local * head_width, head_width)
    share = flat[0] // half_seq

    def own_rows(rows, turn):
        place = 0
        for step in turn:
            place = place * 2 + lax.rem(seq_index // step, 2)
        return lax.dynamic_slice_in_dim(rows, place * share, share, 0)

    def reduced(left, right):
        term = jnp.einsum("hta,htb->hab", left, right, preferred_element_type=jnp.float32)
        return term.astype(jnp.bfloat16).reshape(flat)

    term_gate = reduced(grad_gate, key_rows)
    term_gate, totals = lax.optimization_barrier((term_gate, totals))
    term_up = reduced(grad_up, key_rows)
    term_down = reduced(scaled, hidden_zero)
    term_down, prev_key, prev_value = lax.optimization_barrier((term_down, prev_key, prev_value))
    sums = [term_gate, term_up, term_down]
    for level in range(len(steps)):
        sums = [halved(rows, turn[level]) for rows, turn in zip(sums, turns)]

    keys_all = jnp.concatenate([prev_key, key_rows], axis=1)
    values_all = jnp.concatenate([prev_value, value_rows], axis=1)
    pos_query = offset + jnp.arange(tok_local, dtype=jnp.int32)
    pos_key = offset - WIN + jnp.arange(WIN + tok_local, dtype=jnp.int32)
    allowed = (
        (pos_key[None, :] <= pos_query[:, None])
        & (pos_key[None, :] > pos_query[:, None] - WIN)
        & (pos_key[None, :] >= doc_start[:, None])
    )
    scores = (
        jnp.einsum("hqd,hkd->hqk", query_rows, keys_all, preferred_element_type=jnp.float32)
        * score_scale
    )
    scores = jnp.where(allowed[None], scores, -1e30)
    row_max = jnp.max(scores, axis=-1, keepdims=True)
    expon = jnp.exp(scores - row_max)
    prob_bf = (expon / jnp.sum(expon, axis=-1, keepdims=True)).astype(jnp.bfloat16)
    attended = jnp.einsum(
        "hqk,hkd->hqd", prob_bf, values_all, preferred_element_type=jnp.float32
    ).astype(jnp.bfloat16)

    sums, attended = lax.optimization_barrier((sums, attended))
    inner = 2.0 * update_len / (totals * math.sqrt(update_len * head_width))
    factor = jnp.repeat(inner, head_width)

    def renewed(weight, summed, turn):
        old = own_rows(weight.reshape(flat), turn)
        fresh = renorm_rows(old, summed, own_rows(factor, turn))
        return jnp.where(in_first, old, passed_along(fresh, "seq", half_seq))

    wholes = [renewed(*args) for args in zip((w_gate, w_up, w_down), sums, turns)]
    for level in reversed(range(len(steps))):
        wholes = [doubled(rows, turn[level]) for rows, turn in zip(wholes, turns)]
    use_gate, use_up, use_down = [
        rows.reshape(head_local, head_width, head_width) for rows in wholes
    ]

    query_gate = jnp.einsum("htd,hrd->htr", query_rows, use_gate, preferred_element_type=jnp.float32)
    query_up = jnp.einsum("htd,hrd->htr", query_rows, use_up, preferred_element_type=jnp.float32)
    query_hidden = (query_gate * jax.nn.sigmoid(query_gate) * query_up).astype(jnp.bfloat16)
    query_hidden, use_down = lax.optimization_barrier((query_hidden, use_down))
    fast_out = jnp.einsum(
        "htr,hdr->htd", query_hidden, use_down, preferred_element_type=jnp.float32
    )
    mixed = (attended + fast_out).astype(jnp.bfloat16)
    frame_rows = tok_local // head_count
    head_index = lax.axis_index("head")
    flag_rows = lax.dynamic_slice_in_dim(speech_on, head_index * frame_rows, frame_rows, 0)
    cond_weight = w_cond.reshape(head_local, head_width, cond_width)
    projected = lax.psum_scatter(
        jnp.einsum("htd,hdc->tc", mixed, cond_weight, preferred_element_type=jnp.float32).astype(
            jnp.bfloat16
        ),
        "head",
        scatter_dimension=0,
        tiled=True,
    ).astype(jnp.float32)
    cond = (projected * flag_rows[:, None]).astype(jnp.bfloat16)[None]
    return (mixed, cond)


def solution(mesh):
    placed = (
        P("head", "seq", None),
        P("head", "seq", None),
        P("head", "seq", None),
        P("head", "seq"),
        P("seq"),
        P("seq"),
        P("head", None, None),
        P("head", None, None),
        P("head", None, None),
        P("head", None),
    )
    return jax.shard_map(
        local,
        mesh=mesh,
        in_specs=placed,
        out_specs=(P("head", "seq", None), P("seq", "head", None)),
        check_vma=False,
    )
```
